128 devices in a mesh: row: 16 (over y, z), col: 8 (over x, core).
Axes of the slice: x: 4, y: 4, z: 4, core: 2. Of those that a mesh axis runs over, the one named last changes fastest.
Arguments:
- tokens: bfloat16 [8192, 6144], P('row', 'col'), may hold values from -6 to 6
- weight: bfloat16 [6144, 12288], P('row', 'col'), may hold values from -0.078125 to 0.078125
- cotangent: bfloat16 [8192, 12288], P('row', 'col'), may hold values from -6 to 6
Outputs:
- activated: bfloat16 [8192, 12288], P('row', 'col')
- input_grad: bfloat16 [8192, 6144], P('row', 'col')
The draws below stay inside these ranges and needn't reach their ends.
All inputs are finite; a program needn't handle non-finite values.
Results may differ from the reference program's by a relative error of at most 0.017.
Values may be sent and summed in bfloat16 or wider, within the bound.
A program may use at most 128 MiB of HBM per device.

```python
import math
import jax
import jax.numpy as jnp
from jax import lax

D = 6144
FF = 12288
TOKENS = 8192
N_COL = 8


def levels(rng, shape, split, low, largest):
    gain, own = 1.0, jax.random.fold_in(rng, 6)
    for axis_at, parts in split:
        steps = jnp.exp(jax.random.uniform(jax.random.fold_in(own, axis_at), (parts,), jnp.float32, low / len(split), largest / len(split)))
        gain = gain * jnp.repeat(steps, shape[axis_at] // parts).reshape([-1 if axis == axis_at else 1 for axis in range(len(shape))])
    return gain


def bell_draw(own_key, shape, scale, most, pieces=(), kind=jnp.bfloat16):
    array = scale * jax.random.normal(own_key, shape, jnp.float32)
    if pieces:
        array = array * levels(own_key, shape, pieces, -0.22, 0.18)
    return jnp.clip(array, -most, most).astype(kind)


def setup_inputs(seed: int = 0) -> dict:
    seeds = jax.random.split(jax.random.key(seed), 4)
    return {
        "tokens": bell_draw(seeds[0], (TOKENS, D), 1.0, 6.0, ((0, 16), (1, 8))),
        "weight": bell_draw(seeds[1], (D, FF), D ** -0.5, 0.078125, ((0, 16), (1, 8))),
        "cotangent": bell_draw(seeds[2], (TOKENS, FF), 1.0, 6.0, ((0, 16), (1, 8))),
    }


def gelu_parts(pre):
    cdf = 0.5 * (1.0 + jax.scipy.special.erf(pre / math.sqrt(2.0)))
    pdf = jnp.exp(-0.5 * pre * pre) / math.sqrt(2.0 * math.pi)
    return (pre * cdf, cdf + pre * pdf)

def reference(tokens, weight, cotangent):
    pre = jnp.dot(tokens, weight, preferred_element_type=jnp.float32)
    value, slope = gelu_parts(pre)
    activated = value.astype(jnp.bfloat16)
    grad_pre = (cotangent.astype(jnp.float32) * slope).astype(jnp.bfloat16)
    width = FF // N_COL
    total = jnp.zeros((tokens.shape[0], D), jnp.float32)
    for block in range(N_COL):
        left = grad_pre[:, block * width:(block + 1) * width]
        right = weight[:, block * width:(block + 1) * width]
        partial_b = lax.dot_general(left, right, (((1,), (1,)), ((), ())), preferred_element_type=jnp.float32)
        total = total + partial_b.astype(jnp.bfloat16).astype(jnp.float32)
    return (activated, total.astype(jnp.bfloat16))
```

```python
import functools
import math

import jax
import jax.numpy as jnp
from jax import lax
from jax.experimental import pallas as pl
from jax.experimental.pallas import tpu as pltpu
from jax.sharding import PartitionSpec as P

MESH = pl.DeviceIdType.MESH
RING = 4
CORES = 2
CHUNK = 256


def gelu_parts(pre):
    cdf = 0.5 * (1.0 + lax.erf(pre * (1.0 / math.sqrt(2.0))))
    pdf = jnp.exp(-0.5 * pre * pre) * (1.0 / math.sqrt(2.0 * math.pi))
    return (pre * cdf, cdf + pre * pdf)


def kernel(
    tok_hbm, w_hbm, cot_hbm, act_hbm, grad_hbm,
    tok, w, cot, act, gp, part_out, part_in, staged, first_in, last_in, own, total,
    load_sem, store_sem, w_send, w_recv, t_send, t_recv, d_send, d_recv, x_send, x_recv,
):
    rows, feats = tok_hbm.shape
    depth, width = w_hbm.shape
    chunks = width // CHUNK
    fam = depth // 2
    half = fam // 2
    mid = rows // 2

    r, c = lax.axis_index("row"), lax.axis_index("col")
    y, z = lax.div(r, RING), lax.rem(r, RING)
    x, k = lax.div(c, CORES), lax.rem(c, CORES)

    def at(y, z, x, k):
        return (lax.rem(y, RING) * RING + lax.rem(z, RING), lax.rem(x, RING) * CORES + k)

    neighbours = [
        at(y + 1, z, x, k), at(y + 3, z, x, k), at(y, z + 1, x, k), at(y, z + 3, x, k),
        at(y, z, x + 1, k), at(y, z, x + 3, k), at(y, z, x, 1 - k),
    ]
    x_up, x_down, twin = neighbours[4:]

    def send(src, dst, ssem, rsem, device):
        pltpu.make_async_remote_copy(
            src_ref=src, dst_ref=dst, send_sem=ssem, recv_sem=rsem, device_id=device, device_id_type=MESH
        ).start()

    def arrived(dst, ssem, rsem):
        pltpu.make_async_remote_copy(
            src_ref=dst, dst_ref=dst, send_sem=ssem, recv_sem=rsem, device_id=twin, device_id_type=MESH
        ).wait_recv()

    def sent(src, ssem, rsem):
        pltpu.make_async_remote_copy(
            src_ref=src, dst_ref=src, send_sem=ssem, recv_sem=rsem, device_id=twin, device_id_type=MESH
        ).wait_send()

    def tok_at(x, k, row=0, size=rows):
        return tok.at[pl.ds(row, size), pl.ds(pl.multiple_of((lax.rem(x, RING) * CORES + k) * feats, 128), feats)]

    w_load = pltpu.make_async_copy(w_hbm, w.at[pl.ds(pl.multiple_of(r * depth, 16), depth)], load_sem.at[0])
    w_load.start()
    t_load = pltpu.make_async_copy(tok_hbm, tok_at(x, k), load_sem.at[1])
    t_load.start()
    c_load = pltpu.make_async_copy(cot_hbm, cot, load_sem.at[2])
    c_load.start()

    barrier = pltpu.get_barrier_semaphore()
    for device in neighbours:
        pl.semaphore_signal(barrier, inc=1, device_id=device, device_id_type=MESH)
    pl.semaphore_wait(barrier, len(neighbours))
    w_load.wait()
    t_load.wait()

    def unit(f, p, q, ch, row=0, size=fam):
        ry, rz = (p, q) if f == 0 else (q, p)
        block = lax.rem(ry, RING) * RING + lax.rem(rz, RING)
        return w.at[
            pl.ds(pl.multiple_of(block * depth + f * fam + row, 16), size),
            pl.ds(pl.multiple_of(ch * CHUNK, 128), CHUNK),
        ]

    def family(f):
        if f == 0:
            return y, z, neighbours[0:2], neighbours[2:4]
        return z, y, neighbours[2:4], neighbours[0:2]

    def push(f, ref, ch, index, device):
        send(ref, ref, w_send, w_recv.at[ch, f, index], device)

    def landed(f, ref, ch, index):
        arrived(ref, w_send, w_recv.at[ch, f, index])

    def stage0(ch):
        for f in range(2):
            p, q, ps, qs = family(f)
            for way in range(2):
                push(f, unit(f, p, q, ch), ch, way, ps[way])
        for f in range(2):
            p, q, ps, qs = family(f)
            for way in range(2):
                push(f, unit(f, p, q, ch), ch, 4 + way, qs[way])

    def pass_on(f, ch, j, p):
        _, q, _, qs = family(f)
        for way, step in ((0, -1), (1, 1)):
            landed(f, unit(f, p, q + step + RING, ch), ch, 4 + 2 * j + way)
            push(f, unit(f, p, q + step + RING, ch, way * half, half), ch, 12 + 2 * j + way, qs[way])

    def stage1(ch):
        for f in range(2):
            p, q, ps, qs = family(f)
            for way, step in ((0, -1), (1, 1)):
                there = p + step + RING
                landed(f, unit(f, there, q, ch), ch, way)
                push(f, unit(f, there, q, ch, way * half, half), ch, 2 + way, ps[way])
        for f in range(2):
            p, q, ps, qs = family(f)
            for way, step in ((0, -1), (1, 1)):
                there = p + step + RING
                for way2 in range(2):
                    push(f, unit(f, there, q, ch), ch, 4 + 2 * (1 + way) + way2, qs[way2])
        for f in range(2):
            pass_on(f, ch, 0, family(f)[0])

    def stage2(ch):
        for f in range(2):
            p, q, ps, qs = family(f)
            for way in range(2):
                landed(f, unit(f, p + 2, q, ch, way * half, half), ch, 2 + way)
            for way2 in range(2):
                push(f, unit(f, p + 2, q, ch), ch, 4 + 6 + way2, qs[way2])
        for f in range(2):
            p = family(f)[0]
            pass_on(f, ch, 1, p + 3)
            pass_on(f, ch, 2, p + 1)

    def stage3(ch):
        for f in range(2):
            pass_on(f, ch, 3, family(f)[0] + 2)

    def stage4(ch):
        for f in range(2):
            p, q, ps, qs = family(f)
            for j, there in enumerate((p, p + 3, p + 1, p + 2)):
                for way in range(2):
                    landed(f, unit(f, there, q + 2, ch, way * half, half), ch, 12 + 2 * j + way)

    def tokens0():
        send(tok_at(x, k), tok_at(x, k), t_send, t_recv.at[0], x_up)
        send(tok_at(x, k), tok_at(x, k), t_send, t_recv.at[1], x_down)
        send(tok_at(x, k), tok_at(x, k), t_send, t_recv.at[4], twin)

    def tokens1():
        for way, there, device in ((0, x + 3, x_up), (1, x + 1, x_down)):
            arrived(tok_at(there, k), t_send, t_recv.at[way])
            piece = tok_at(there, k, way * mid, mid)
            send(piece, piece, t_send, t_recv.at[2 + way], device)
            send(tok_at(there, k), tok_at(there, k), t_send, t_recv.at[5 + way], twin)

    def tokens2():
        for way in range(2):
            arrived(tok_at(x + 2, k, way * mid, mid), t_send, t_recv.at[2 + way])
        send(tok_at(x + 2, k), tok_at(x + 2, k), t_send, t_recv.at[7], twin)

    def tokens3():
        for j, there in enumerate((x, x + 3, x + 1, x + 2)):
            arrived(tok_at(there, 1 - k), t_send, t_recv.at[4 + j])

    def store(ch):
        columns = pl.ds(pl.multiple_of(ch * CHUNK, 128), CHUNK)
        return pltpu.make_async_copy(act.at[:, columns], act_hbm.at[:, columns], store_sem.at[ch])

    def compute(ch):
        columns = pl.ds(pl.multiple_of(ch * CHUNK, 128), CHUNK)
        step = rows // 2

        def body(i, _):
            these = pl.ds(pl.multiple_of(i * step, 16), step)
            pre = jnp.dot(tok[these, :], w[:, columns], preferred_element_type=jnp.float32)
            value, slope = gelu_parts(pre)
            act[these, columns] = value.astype(jnp.bfloat16)
            gp[these, columns] = (cot[these, columns].astype(jnp.float32) * slope).astype(jnp.bfloat16)
            return 0

        lax.fori_loop(0, 2, body, 0)
        store(ch).start()

    def tick(t, _):
        for lag, stage in ((3, stage3), (2, stage2), (1, stage1), (0, stage0)):
            @pl.when((t >= lag) & (t - lag < chunks))
            def _():
                stage(t - lag)

        for at_tick, stage in ((0, tokens0), (1, tokens1), (2, tokens2), (4, tokens3)):
            @pl.when(t == at_tick)
            def _():
                stage()

        @pl.when(t == 4)
        def _():
            c_load.wait()

        @pl.when(t >= 4)
        def _():
            stage4(t - 4)
            compute(t - 4)

        return 0

    lax.fori_loop(0, chunks + 4, tick, 0)

    sent(tok.at[:, pl.ds(0, (2 * RING - 1) * feats)], t_send, t_send)

    steps = ((2, 0), (2, 1), (1, 1), (3, 0), (1, 0), (3, 1), (0, 0), (0, 1))

    def product(dx, h, core, dst):
        tile = 256

        def body(n, _):
            start = (lax.rem(x + dx, RING) * CORES + core) * feats + n * tile
            part = lax.dot_general(
                gp[pl.ds(h * mid, mid), :],
                w[pl.ds(pl.multiple_of(start, 128), tile), :],
                (((1,), (1,)), ((), ())),
                preferred_element_type=jnp.float32,
            )
            dst[:, pl.ds(pl.multiple_of(n * tile, 128), tile)] = part.astype(dst.dtype)
            return 0

        lax.fori_loop(0, feats // tile, body, 0)

    def for_twin(s):
        dx, h = steps[s]
        product(dx, h, 1 - k, part_out.at[s])
        send(part_out.at[s], part_in.at[s], d_send.at[s], d_recv.at[s], twin)

    for_twin(0)
    for s, (dx, h) in enumerate(steps):
        if s + 1 < len(steps):
            for_twin(s + 1)
        mine = own.at[pl.ds(h * mid, mid)] if dx == 0 else total
        product(dx, h, k, mine)
        arrived(part_in.at[s], d_send.at[s], d_recv.at[s])
        if dx == 0:
            mine[...] = mine[...] + part_in[s].astype(jnp.float32)
            continue
        summed = mine[...] + part_in[s].astype(jnp.float32)
        if dx == 2:
            staged[s] = summed.astype(jnp.bfloat16)
            send(staged.at[s], first_in.at[h], x_send.at[s], x_recv.at[s], x_up if h == 0 else x_down)
            continue
        way = 0 if dx == 1 else 1
        if h == way:
            arrived(first_in.at[way], x_send.at[way], x_recv.at[way])
            summed = summed + first_in[way].astype(jnp.float32)
        staged[s] = summed.astype(jnp.bfloat16)
        send(staged.at[s], last_in.at[way, h], x_send.at[s], x_recv.at[s], x_up if way == 0 else x_down)

    out_dma = []
    for h in (1, 0):
        s_up = steps.index((1, h))
        s_down = steps.index((3, h))
        arrived(last_in.at[0, h], x_send.at[s_up], x_recv.at[s_up])
        arrived(last_in.at[1, h], x_send.at[s_down], x_recv.at[s_down])
        these = pl.ds(h * mid, mid)
        result = own[these, :] + last_in[0, h].astype(jnp.float32) + last_in[1, h].astype(jnp.float32)
        tok[these, pl.ds(0, feats)] = result.astype(jnp.bfloat16)
        copy = pltpu.make_async_copy(tok.at[these, pl.ds(0, feats)], grad_hbm.at[these, :], load_sem.at[h])
        copy.start()
        out_dma.append(copy)

    for copy in out_dma:
        copy.wait()

    def stored(ch, _):
        store(ch).wait()
        return 0

    lax.fori_loop(0, chunks, stored, 0)
    for s in range(6):
        sent(staged.at[s], x_send.at[s], x_recv.at[s])
    for s in range(8):
        sent(part_out.at[s], d_send.at[s], d_recv.at[s])
    ring = RING * RING - 1
    sent(w.at[pl.ds(0, ring * depth)], w_send, w_send)


def solution(mesh):
    def local(tokens, weight, cotangent):
        rows, feats = tokens.shape
        depth, width = weight.shape
        n_row, n_col = mesh.shape["row"], mesh.shape["col"]
        chunks = width // CHUNK
        mid = rows // 2
        bf16, f32 = jnp.bfloat16, jnp.float32
        dma = pltpu.SemaphoreType.DMA
        return pl.pallas_call(
            kernel,
            out_shape=(
                jax.ShapeDtypeStruct((rows, width), bf16),
                jax.ShapeDtypeStruct((rows, feats), bf16),
            ),
            in_specs=[pl.BlockSpec(memory_space=pl.ANY)] * 3,
            out_specs=(pl.BlockSpec(memory_space=pl.ANY),) * 2,
            scratch_shapes=[
                pltpu.VMEM((rows, feats * n_col), bf16),
                pltpu.VMEM((depth * n_row, width), bf16),
                pltpu.VMEM((rows, width), bf16),
                pltpu.VMEM((rows, width), bf16),
                pltpu.VMEM((rows, width), bf16),
                pltpu.VMEM((8, mid, feats), bf16),
                pltpu.VMEM((8, mid, feats), bf16),
                pltpu.VMEM((6, mid, feats), bf16),
                pltpu.VMEM((2, mid, feats), bf16),
                pltpu.VMEM((2, 2, mid, feats), bf16),
                pltpu.VMEM((rows, feats), f32),
                pltpu.VMEM((mid, feats), f32),
                dma((3,)),
                dma((chunks,)),
                dma,
                dma((chunks, 2, 20)),
                dma,
                dma((8,)),
                dma((8,)),
                dma((8,)),
                dma((6,)),
                dma((6,)),
            ],
            compiler_params=pltpu.CompilerParams(
                collective_id=0, has_side_effects=True, vmem_limit_bytes=60 << 20
            ),
            cost_estimate=pl.CostEstimate(
                flops=4 * rows * feats * n_col * width, bytes_accessed=1 << 24, transcendentals=2 * rows * width
            ),
        )(tokens, weight, cotangent)

    in_specs = (P("row", "col"), P("row", "col"), P("row", "col"))
    out_specs = (P("row", "col"), P("row", "col"))
    return jax.shard_map(local, mesh=mesh, in_specs=in_specs, out_specs=out_specs, check_vma=False)
```

```python
import functools
import math

import jax
import jax.numpy as jnp
from jax import lax
from jax.experimental import pallas as pl
from jax.experimental.pallas import tpu as pltpu
from jax.sharding import PartitionSpec as P

MESH = pl.DeviceIdType.MESH
RING = 4
CORES = 2
WIDTHS = (512, 512, 512)
STARTS = tuple(sum(WIDTHS[:i]) for i in range(len(WIDTHS)))
STEPS = ((2, 0), (2, 1), (1, 1), (3, 0), (1, 0), (3, 1), (0, 0), (0, 1))
EARLY = 2
EARLY_CHUNKS, EARLY_TICK = 1, 4

def gelu_parts(pre):
    cdf = 0.5 * (1.0 + lax.erf(pre * (1.0 / math.sqrt(2.0))))
    pdf = jnp.exp(-0.5 * pre * pre) * (1.0 / math.sqrt(2.0 * math.pi))
    return (pre * cdf, cdf + pre * pdf)


def kernel(
    tok_hbm, w_hbm, cot_hbm, act_hbm, grad_hbm,
    tok, ws, cot, pre, act, gp, part_out, part_in, staged, first_in, last_in, begun, own, total,
    load_sem, w_sem, store_sem, w_send, w_recv, t_send, t_recv, d_send, d_recv, x_send, x_recv, g_sem,
):
    rows, feats = tok_hbm.shape
    depth, width = w_hbm.shape
    chunks = len(WIDTHS)
    fam = depth // 2
    half = fam // 2
    mid = rows // 2

    r, c = lax.axis_index("row"), lax.axis_index("col")
    y, z = lax.div(r, RING), lax.rem(r, RING)
    x, k = lax.div(c, CORES), lax.rem(c, CORES)

    def at(y, z, x, k):
        return (lax.rem(y, RING) * RING + lax.rem(z, RING), lax.rem(x, RING) * CORES + k)

    neighbours = [
        at(y + 1, z, x, k), at(y + 3, z, x, k), at(y, z + 1, x, k), at(y, z + 3, x, k),
        at(y, z, x + 1, k), at(y, z, x + 3, k), at(y, z, x, 1 - k),
    ]
    x_up, x_down, twin = neighbours[4:]

    def send(src, dst, ssem, rsem, device):
        pltpu.make_async_remote_copy(
            src_ref=src, dst_ref=dst, send_sem=ssem, recv_sem=rsem, device_id=device, device_id_type=MESH
        ).start()

    def arrived(dst, ssem, rsem):
        pltpu.make_async_remote_copy(
            src_ref=dst, dst_ref=dst, send_sem=ssem, recv_sem=rsem, device_id=twin, device_id_type=MESH
        ).wait_recv()

    def sent(src, ssem, rsem):
        pltpu.make_async_remote_copy(
            src_ref=src, dst_ref=src, send_sem=ssem, recv_sem=rsem, device_id=twin, device_id_type=MESH
        ).wait_send()

    def tok_at(x, k, row=0, size=rows):
        return tok.at[pl.ds(row, size), pl.ds(pl.multiple_of((lax.rem(x, RING) * CORES + k) * feats, 128), feats)]

    def w_load(ch):
        return pltpu.make_async_copy(
            w_hbm.at[:, pl.ds(STARTS[ch], WIDTHS[ch])],
            ws[ch].at[pl.ds(pl.multiple_of(r * depth, 16), depth)],
            w_sem.at[ch],
        )

    for ch in range(chunks):
        w_load(ch).start()
    def t_load():
        return pltpu.make_async_copy(tok_hbm, tok_at(x, k), load_sem.at[1])

    def c_load():
        return pltpu.make_async_copy(cot_hbm, cot, load_sem.at[2])

    t_load().start()
    c_load().start()

    barrier = pltpu.get_barrier_semaphore()
    for device in neighbours:
        pl.semaphore_signal(barrier, inc=1, device_id=device, device_id_type=MESH)
    pl.semaphore_wait(barrier, len(neighbours))

    at_block = [
        [pl.multiple_of((lax.rem(y + dy, RING) * RING + lax.rem(z + dz, RING)) * depth, 16) for dz in range(RING)]
        for dy in range(RING)
    ]
    ring_y, ring_z = neighbours[0:2], neighbours[2:4]

    def unit(f, dp, dq, ch, row=0, size=fam):
        dy, dz = (dp, dq) if f == 0 else (dq, dp)
        return ws[ch].at[pl.ds(at_block[dy % RING][dz % RING] + (f * fam + row), size)]

    def parts(f, ch, n):
        way = n % 2
        back = (-1, 1)[way]
        first, second = (ring_y, ring_z) if f == 0 else (ring_z, ring_y)
        cut = (way * half, half)
        if n < 2:
            return unit(f, 0, 0, ch), unit(f, back, 0, ch), first[way]
        if n < 4:
            return unit(f, back, 0, ch, *cut), unit(f, 2, 0, ch, *cut), first[way]
        place = (0, -1, 1, 2)[(n - 4) % 8 // 2]
        if n < 12:
            return unit(f, place, 0, ch), unit(f, place, back, ch), second[way]
        return unit(f, place, back, ch, *cut), unit(f, place, 2, ch, *cut), second[way]

    def push(f, ch, *ns):
        for n in ns:
            out, _, device = parts(f, ch, n)
            send(out, out, w_send.at[ch], w_recv.at[ch, f, n], device)

    def landed(f, ch, *ns):
        for n in ns:
            arrived(parts(f, ch, n)[1], w_send.at[ch], w_recv.at[ch, f, n])

    def stage0(ch):
        w_load(ch).wait()
        for f in range(2):
            push(f, ch, 0, 1)
        for f in range(2):
            push(f, ch, 4, 5)

    def stage1(f, ch):
        for way in range(2):
            landed(f, ch, way)
            push(f, ch, 2 + way, 6 + 2 * way, 7 + 2 * way)
        for way in range(2):
            landed(f, ch, 4 + way)
            push(f, ch, 12 + way)

    def stage2(f, ch):
        landed(f, ch, 2, 3)
        push(f, ch, 10, 11)
        for n in (6, 7, 8, 9):
            landed(f, ch, n)
            push(f, ch, 8 + n)

    def stage3(f, ch):
        for n in (10, 11):
            landed(f, ch, n)
            push(f, ch, 8 + n)

    ends = ((), (), (12, 13), (14, 15, 16, 17), (18, 19))

    blocks = (
        ((0, 0),),
        ((1, 0), (3, 0), (0, 1), (0, 3)),
        ((2, 0), (0, 2), (1, 1), (1, 3), (3, 1), (3, 3)),
        ((1, 2), (3, 2), (2, 1), (2, 3)),
        ((2, 2),),
    )

    def accumulate(ch, stage):
        columns = pl.ds(STARTS[ch], WIDTHS[ch])
        for f in range(2):
            landed(f, ch, *ends[stage])

        for dy, dz in blocks[stage]:
            there = pl.ds(at_block[dy][dz], depth)

            def body(i, _):
                these = pl.ds(pl.multiple_of(i * mid, 16), mid)
                part = jnp.dot(tok[these, there], ws[ch][there, :], preferred_element_type=jnp.float32)
                pre[these, columns] = part if stage == 0 else pre[these, columns] + part
                return 0

            lax.fori_loop(0, 2, body, 0)

    def tokens0():
        send(tok_at(x, k), tok_at(x, k), t_send, t_recv.at[0], x_up)
        send(tok_at(x, k), tok_at(x, k), t_send, t_recv.at[1], x_down)
        send(tok_at(x, k), tok_at(x, k), t_send, t_recv.at[4], twin)

    def tokens1():
        for way, there, device in ((0, x + 3, x_up), (1, x + 1, x_down)):
            arrived(tok_at(there, k), t_send, t_recv.at[way])
            piece = tok_at(there, k, way * mid, mid)
            send(piece, piece, t_send, t_recv.at[2 + way], device)
            send(tok_at(there, k), tok_at(there, k), t_send, t_recv.at[5 + way], twin)

    def tokens2():
        for way in range(2):
            arrived(tok_at(x + 2, k, way * mid, mid), t_send, t_recv.at[2 + way])
        send(tok_at(x + 2, k), tok_at(x + 2, k), t_send, t_recv.at[7], twin)

    def tokens3():
        for j, there in enumerate((x, x + 3, x + 1, x + 2)):
            arrived(tok_at(there, 1 - k), t_send, t_recv.at[4 + j])

    def store(ch):
        columns = pl.ds(STARTS[ch], WIDTHS[ch])
        return pltpu.make_async_copy(act.at[:, columns], act_hbm.at[:, columns], store_sem.at[ch])

    def activate(ch):
        columns = pl.ds(STARTS[ch], WIDTHS[ch])
        step = rows // 4

        def body(i, _):
            these = pl.ds(pl.multiple_of(i * step, 16), step)
            value, slope = gelu_parts(pre[these, columns])
            act[these, columns] = value.astype(jnp.bfloat16)
            gp[these, columns] = (cot[these, columns].astype(jnp.float32) * slope).astype(jnp.bfloat16)
            return 0

        lax.fori_loop(0, 4, body, 0)
        store(ch).start()

    def product(s, core, dst, chs, begun=None):
        dx, h = STEPS[s]
        tile = 256

        def body(n, _):
            begin = (lax.rem(x + dx, RING) * CORES + core) * feats + n * tile
            columns = pl.ds(pl.multiple_of(n * tile, 128), tile)
            part = 0.0 if begun is None else begun[:, columns]
            for ch in chs:
                part += lax.dot_general(
                    gp[pl.ds(h * mid, mid), pl.ds(STARTS[ch], WIDTHS[ch])],
                    ws[ch][pl.ds(pl.multiple_of(begin, 128), tile), :],
                    (((1,), (1,)), ((), ())),
                    preferred_element_type=jnp.float32,
                )
            dst[:, columns] = part.astype(dst.dtype)
            return 0

        lax.fori_loop(0, feats // tile, body, 0)

    chs = tuple(range(chunks))
    stages = (None, stage1, stage2, stage3)
    behind = []
    stage0(0)
    t_load().wait()
    tokens0()
    if chunks > 1:
        stage0(1)
    behind += [(ch, 0) for ch in range(chunks)]
    for t in range(1, chunks + 4):
        for lag in (3, 2, 1):
            for f in range(2):
                if 0 <= t - lag < chunks:
                    stages[lag](f, t - lag)
        if t + 1 < chunks:
            stage0(t + 1)
        behind += [(t - lag, lag) for lag in (3, 2, 1) if 0 <= t - lag < chunks]
        if t == 1:
            tokens1()
            tokens2()
        if t == 2:
            tokens3()
            c_load().wait()
        if t >= 2:
            for ch, stage in sorted(behind):
                accumulate(ch, stage)
            behind = []
        if t >= 4:
            accumulate(t - 4, 4)
            activate(t - 4)
        if t == EARLY_TICK:
            for n in range(2 * EARLY):
                product(n // 2, (1 - k, k)[n % 2], begun.at[n], chs[:EARLY_CHUNKS])

    sent(tok.at[:, pl.ds(0, (2 * RING - 1) * feats)], t_send, t_send)

    def finish(s, n, core, dst):
        if s < EARLY:
            product(s, core, dst, chs[EARLY_CHUNKS:], begun.at[2 * s + n])
        else:
            product(s, core, dst, chs)

    def for_twin(s):
        finish(s, 0, 1 - k, part_out.at[s])
        send(part_out.at[s], part_in.at[s], d_send.at[s], d_recv.at[s], twin)

    for s in range(EARLY):
        for_twin(s)
    for s, (dx, h) in enumerate(STEPS):
        for later in range(EARLY, 4) if s == 2 else (s + 1,) if s > 2 else ():
            if later < len(STEPS):
                for_twin(later)
        mine = own.at[pl.ds(h * mid, mid)] if dx == 0 else total
        finish(s, 1, k, mine)
        arrived(part_in.at[s], d_send.at[s], d_recv.at[s])
        summed = mine[...] + part_in[s].astype(jnp.float32)
        if dx == 0:
            mine[...] = summed
            continue
        way = h if dx == 2 else dx // 2
        if dx != 2 and h == way:
            arrived(first_in.at[way], x_send.at[way], x_recv.at[way])
            summed = summed + first_in[way].astype(jnp.float32)
        staged[s] = summed.astype(jnp.bfloat16)
        into = first_in.at[h] if dx == 2 else last_in.at[way, h]
        send(staged.at[s], into, x_send.at[s], x_recv.at[s], (x_up, x_down)[way])

    out_dma = []
    for h in range(2):
        for way, dx in enumerate((1, 3)):
            s = STEPS.index((dx, h))
            arrived(last_in.at[way, h], x_send.at[s], x_recv.at[s])
        these = pl.ds(h * mid, mid)
        result = own[these, :] + last_in[0, h].astype(jnp.float32) + last_in[1, h].astype(jnp.float32)
        tok[these, pl.ds(0, feats)] = result.astype(jnp.bfloat16)
        copy = pltpu.make_async_copy(tok.at[these, pl.ds(0, feats)], grad_hbm.at[these, :], g_sem.at[h])
        copy.start()
        out_dma.append(copy)

    for copy in out_dma:
        copy.wait()

    for ch in range(chunks):
        store(ch).wait()
    for s, (dx, _) in enumerate(STEPS):
        sent(part_out.at[s], d_send.at[s], d_recv.at[s])
        if dx:
            sent(staged.at[s], x_send.at[s], x_recv.at[s])
    ring = RING * RING - 1
    for ch in range(chunks):
        sent(ws[ch].at[pl.ds(0, ring * depth)], w_send.at[ch], w_send.at[ch])


def solution(mesh):
    def local(tokens, weight, cotangent):
        rows, feats = tokens.shape
        depth, width = weight.shape
        n_row, n_col = mesh.shape["row"], mesh.shape["col"]
        chunks = len(WIDTHS)
        mid = rows // 2
        bf16, f32 = jnp.bfloat16, jnp.float32
        dma = pltpu.SemaphoreType.DMA
        return pl.pallas_call(
            kernel,
            out_shape=(
                jax.ShapeDtypeStruct((rows, width), bf16),
                jax.ShapeDtypeStruct((rows, feats), bf16),
            ),
            in_specs=[pl.BlockSpec(memory_space=pl.ANY)] * 3,
            out_specs=(pl.BlockSpec(memory_space=pl.ANY),) * 2,
            scratch_shapes=[
                pltpu.VMEM((rows, feats * n_col), bf16),
                tuple(pltpu.VMEM((depth * n_row, size), bf16) for size in WIDTHS),
                pltpu.VMEM((rows, width), bf16),
                pltpu.VMEM((rows, width), f32),
                pltpu.VMEM((rows, width), bf16),
                pltpu.VMEM((rows, width), bf16),
                pltpu.VMEM((8, mid, feats), bf16),
                pltpu.VMEM((8, mid, feats), bf16),
                pltpu.VMEM((6, mid, feats), bf16),
                pltpu.VMEM((2, mid, feats), bf16),
                pltpu.VMEM((2, 2, mid, feats), bf16),
                pltpu.VMEM((2 * EARLY, mid, feats), f32),
                pltpu.VMEM((rows, feats), f32),
                pltpu.VMEM((mid, feats), f32),
                dma((3,)),
                dma((chunks,)),
                dma((chunks,)),
                dma((chunks,)),
                dma((chunks, 2, 20)),
                dma,
                dma((8,)),
                dma((len(STEPS),)),
                dma((len(STEPS),)),
                dma((len(STEPS),)),
                dma((len(STEPS),)),
                dma((2,)),
            ],
            compiler_params=pltpu.CompilerParams(
                collective_id=0, has_side_effects=True, vmem_limit_bytes=60 << 20
            ),
            cost_estimate=pl.CostEstimate(
                flops=4 * rows * feats * n_col * width, bytes_accessed=1 << 24, transcendentals=2 * rows * width
            ),
        )(tokens, weight, cotangent)

    in_specs = (P("row", "col"), P("row", "col"), P("row", "col"))
    out_specs = (P("row", "col"), P("row", "col"))
    return jax.shard_map(local, mesh=mesh, in_specs=in_specs, out_specs=out_specs, check_vma=False)
```

```python
import functools
import math

import jax
import jax.numpy as jnp
from jax import lax
from jax.experimental import pallas as pl
from jax.experimental.pallas import tpu as pltpu
from jax.sharding import PartitionSpec as P

MESH = pl.DeviceIdType.MESH
RING = 4
CORES = 2
WIDTHS = (512, 512, 512)
STARTS = tuple(sum(WIDTHS[:i]) for i in range(len(WIDTHS)))
STEPS = ((2, 0), (2, 1), (1, 1), (3, 0), (1, 0), (3, 1), (0, 0), (0, 1))
EARLY = 2
EARLY_CHUNKS, EARLY_TICK = 1, 4

def gelu_parts(pre):
    cdf = 0.5 * (1.0 + lax.erf(pre * (1.0 / math.sqrt(2.0))))
    pdf = jnp.exp(-0.5 * pre * pre) * (1.0 / math.sqrt(2.0 * math.pi))
    return (pre * cdf, cdf + pre * pdf)


def kernel(
    tok_hbm, w_hbm, cot_hbm, act, grad,
    tok, ws, cot, pre, gp, part_out, part_in, staged, first_in, last_in, begun, own, total,
    load_sem, w_sem, w_send, w_recv, t_send, t_recv, d_send, d_recv, x_send, x_recv,
):
    rows, feats = tok_hbm.shape
    depth, width = w_hbm.shape
    chunks = len(WIDTHS)
    fam = depth // 2
    half = fam // 2
    mid = rows // 2

    r, c = lax.axis_index("row"), lax.axis_index("col")
    y, z = lax.div(r, RING), lax.rem(r, RING)
    x, k = lax.div(c, CORES), lax.rem(c, CORES)

    def at(y, z, x, k):
        return (lax.rem(y, RING) * RING + lax.rem(z, RING), lax.rem(x, RING) * CORES + k)

    neighbours = [
        at(y + 1, z, x, k), at(y + 3, z, x, k), at(y, z + 1, x, k), at(y, z + 3, x, k),
        at(y, z, x + 1, k), at(y, z, x + 3, k), at(y, z, x, 1 - k),
    ]
    x_up, x_down, twin = neighbours[4:]

    def send(src, dst, ssem, rsem, device):
        pltpu.make_async_remote_copy(
            src_ref=src, dst_ref=dst, send_sem=ssem, recv_sem=rsem, device_id=device, device_id_type=MESH
        ).start()

    def arrived(dst, ssem, rsem):
        pltpu.make_async_remote_copy(
            src_ref=dst, dst_ref=dst, send_sem=ssem, recv_sem=rsem, device_id=twin, device_id_type=MESH
        ).wait_recv()

    def sent(src, ssem, rsem):
        pltpu.make_async_remote_copy(
            src_ref=src, dst_ref=src, send_sem=ssem, recv_sem=rsem, device_id=twin, device_id_type=MESH
        ).wait_send()

    def tok_at(x, k, row=0, size=rows):
        return tok.at[pl.ds(row, size), pl.ds(pl.multiple_of((lax.rem(x, RING) * CORES + k) * feats, 128), feats)]

    def w_load(ch):
        return pltpu.make_async_copy(
            w_hbm.at[:, pl.ds(STARTS[ch], WIDTHS[ch])],
            ws[ch].at[pl.ds(pl.multiple_of(r * depth, 16), depth)],
            w_sem.at[ch],
        )

    for ch in range(chunks):
        w_load(ch).start()
    def t_load():
        return pltpu.make_async_copy(tok_hbm, tok_at(x, k), load_sem.at[1])

    def c_load():
        return pltpu.make_async_copy(cot_hbm, cot, load_sem.at[2])

    t_load().start()
    c_load().start()

    barrier = pltpu.get_barrier_semaphore()
    for device in neighbours:
        pl.semaphore_signal(barrier, inc=1, device_id=device, device_id_type=MESH)
    pl.semaphore_wait(barrier, len(neighbours))

    at_block = [
        [pl.multiple_of((lax.rem(y + dy, RING) * RING + lax.rem(z + dz, RING)) * depth, 16) for dz in range(RING)]
        for dy in range(RING)
    ]
    ring_y, ring_z = neighbours[0:2], neighbours[2:4]

    def unit(f, dp, dq, ch, row=0, size=fam):
        dy, dz = (dp, dq) if f == 0 else (dq, dp)
        return ws[ch].at[pl.ds(at_block[dy % RING][dz % RING] + (f * fam + row), size)]

    def parts(f, ch, n):
        way = n % 2
        back = (-1, 1)[way]
        first, second = (ring_y, ring_z) if f == 0 else (ring_z, ring_y)
        cut = (way * half, half)
        if n < 2:
            return unit(f, 0, 0, ch), unit(f, back, 0, ch), first[way]
        if n < 4:
            return unit(f, back, 0, ch, *cut), unit(f, 2, 0, ch, *cut), first[way]
        place = (0, -1, 1, 2)[(n - 4) % 8 // 2]
        if n < 12:
            return unit(f, place, 0, ch), unit(f, place, back, ch), second[way]
        return unit(f, place, back, ch, *cut), unit(f, place, 2, ch, *cut), second[way]

    def push(f, ch, *ns):
        for n in ns:
            out, _, device = parts(f, ch, n)
            send(out, out, w_send.at[ch], w_recv.at[ch, f, n], device)

    def landed(f, ch, *ns):
        for n in ns:
            arrived(parts(f, ch, n)[1], w_send.at[ch], w_recv.at[ch, f, n])

    def stage0(ch):
        w_load(ch).wait()
        for f in range(2):
            push(f, ch, 0, 1)
        for f in range(2):
            push(f, ch, 4, 5)

    def stage1(f, ch):
        for way in range(2):
            landed(f, ch, way)
            push(f, ch, 2 + way, 6 + 2 * way, 7 + 2 * way)
        for way in range(2):
            landed(f, ch, 4 + way)
            push(f, ch, 12 + way)

    def stage2(f, ch):
        landed(f, ch, 2, 3)
        push(f, ch, 10, 11)
        for n in (6, 7, 8, 9):
            landed(f, ch, n)
            push(f, ch, 8 + n)

    def stage3(f, ch):
        for n in (10, 11):
            landed(f, ch, n)
            push(f, ch, 8 + n)

    ends = ((), (), (12, 13), (14, 15, 16, 17), (18, 19))

    blocks = (
        ((0, 0),),
        ((1, 0), (3, 0), (0, 1), (0, 3)),
        ((2, 0), (0, 2), (1, 1), (1, 3), (3, 1), (3, 3)),
        ((1, 2), (3, 2), (2, 1), (2, 3)),
        ((2, 2),),
    )

    def accumulate(ch, stage):
        columns = pl.ds(STARTS[ch], WIDTHS[ch])
        for f in range(2):
            landed(f, ch, *ends[stage])

        for dy, dz in blocks[stage]:
            there = pl.ds(at_block[dy][dz], depth)

            def body(i, _):
                these = pl.ds(pl.multiple_of(i * mid, 16), mid)
                part = jnp.dot(tok[these, there], ws[ch][there, :], preferred_element_type=jnp.float32)
                pre[these, columns] = part if stage == 0 else pre[these, columns] + part
                return 0

            lax.fori_loop(0, 2, body, 0)

    def tokens0():
        send(tok_at(x, k), tok_at(x, k), t_send, t_recv.at[0], x_up)
        send(tok_at(x, k), tok_at(x, k), t_send, t_recv.at[1], x_down)
        send(tok_at(x, k), tok_at(x, k), t_send, t_recv.at[4], twin)

    def tokens1():
        for way, there, device in ((0, x + 3, x_up), (1, x + 1, x_down)):
            arrived(tok_at(there, k), t_send, t_recv.at[way])
            piece = tok_at(there, k, way * mid, mid)
            send(piece, piece, t_send, t_recv.at[2 + way], device)
            send(tok_at(there, k), tok_at(there, k), t_send, t_recv.at[5 + way], twin)

    def tokens2():
        for way in range(2):
            arrived(tok_at(x + 2, k, way * mid, mid), t_send, t_recv.at[2 + way])
        send(tok_at(x + 2, k), tok_at(x + 2, k), t_send, t_recv.at[7], twin)

    def tokens3():
        for j, there in enumerate((x, x + 3, x + 1, x + 2)):
            arrived(tok_at(there, 1 - k), t_send, t_recv.at[4 + j])

    def activate(ch, half_from):
        columns = pl.ds(STARTS[ch], WIDTHS[ch])
        step = rows // 4

        def body(i, _):
            these = pl.ds(pl.multiple_of(i * step, 16), step)
            value, slope = gelu_parts(pre[these, columns])
            act[these, columns] = value.astype(jnp.bfloat16)
            gp[these, columns] = (cot[these, columns].astype(jnp.float32) * slope).astype(jnp.bfloat16)
            return 0

        lax.fori_loop(half_from * 2, half_from * 2 + 2, body, 0)

    def product(s, core, dst, chs, begun=None):
        dx, h = STEPS[s]
        tile = 256

        def body(n, _):
            begin = (lax.rem(x + dx, RING) * CORES + core) * feats + n * tile
            columns = pl.ds(pl.multiple_of(n * tile, 128), tile)
            part = 0.0 if begun is None else begun[:, columns]
            for ch in chs:
                part += lax.dot_general(
                    gp[pl.ds(h * mid, mid), pl.ds(STARTS[ch], WIDTHS[ch])],
                    ws[ch][pl.ds(pl.multiple_of(begin, 128), tile), :],
                    (((1,), (1,)), ((), ())),
                    preferred_element_type=jnp.float32,
                )
            dst[:, columns] = part.astype(dst.dtype)
            return 0

        lax.fori_loop(0, feats // tile, body, 0)

    chs = tuple(range(chunks))
    stages = (None, stage1, stage2, stage3)
    behind = []
    stage0(0)
    t_load().wait()
    tokens0()
    if chunks > 1:
        stage0(1)
    behind += [(ch, 0) for ch in range(chunks)]
    for t in range(1, chunks + 4):
        for lag in (3, 2, 1):
            for f in range(2):
                if 0 <= t - lag < chunks:
                    stages[lag](f, t - lag)
        if t + 1 < chunks:
            stage0(t + 1)
        behind += [(t - lag, lag) for lag in (3, 2, 1) if 0 <= t - lag < chunks]
        if t == 1:
            tokens1()
            tokens2()
        if t == 2:
            tokens3()
            c_load().wait()
        if t >= 2:
            for ch, stage in sorted(behind):
                accumulate(ch, stage)
            behind = []
        if t >= 4:
            accumulate(t - 4, 4)
            if t < chunks + 3:
                activate(t - 4, 0)
                activate(t - 4, 1)
        if t == EARLY_TICK:
            for n in range(2 * EARLY):
                product(n // 2, (1 - k, k)[n % 2], begun.at[n], chs[:EARLY_CHUNKS])

    sent(tok.at[:, pl.ds(0, (2 * RING - 1) * feats)], t_send, t_send)

    def finish(s, n, core, dst):
        if s < EARLY:
            product(s, core, dst, chs[EARLY_CHUNKS:], begun.at[2 * s + n])
        else:
            product(s, core, dst, chs)

    def for_twin(s):
        finish(s, 0, 1 - k, part_out.at[s])
        send(part_out.at[s], part_in.at[s], d_send.at[s], d_recv.at[s], twin)

    for s in range(EARLY):
        activate(chunks - 1, s)
        for_twin(s)
    for s, (dx, h) in enumerate(STEPS):
        for later in range(EARLY, 4) if s == 2 else (s + 1,) if s > 2 else ():
            if later < len(STEPS):
                for_twin(later)
        mine = own.at[pl.ds(h * mid, mid)] if dx == 0 else total
        finish(s, 1, k, mine)
        arrived(part_in.at[s], d_send.at[s], d_recv.at[s])
        summed = mine[...] + part_in[s].astype(jnp.float32)
        if dx == 0:
            mine[...] = summed
            continue
        way = h if dx == 2 else dx // 2
        if dx != 2 and h == way:
            arrived(first_in.at[way], x_send.at[way], x_recv.at[way])
            summed = summed + first_in[way].astype(jnp.float32)
        staged[s] = summed.astype(jnp.bfloat16)
        into = first_in.at[h] if dx == 2 else last_in.at[way, h]
        send(staged.at[s], into, x_send.at[s], x_recv.at[s], (x_up, x_down)[way])

    for h in range(2):
        for way, dx in enumerate((1, 3)):
            s = STEPS.index((dx, h))
            arrived(last_in.at[way, h], x_send.at[s], x_recv.at[s])
        for i in range(2):
            size = mid // 2
            these, inner = pl.ds(h * mid + i * size, size), pl.ds(i * size, size)
            result = own[these, :] + last_in[0, h, inner].astype(jnp.float32) + last_in[1, h, inner].astype(jnp.float32)
            grad[these, :] = result.astype(jnp.bfloat16)

    for s, (dx, _) in enumerate(STEPS):
        sent(part_out.at[s], d_send.at[s], d_recv.at[s])
        if dx:
            sent(staged.at[s], x_send.at[s], x_recv.at[s])
    ring = RING * RING - 1
    for ch in range(chunks):
        sent(ws[ch].at[pl.ds(0, ring * depth)], w_send.at[ch], w_send.at[ch])


def hand_on(act_in, grad_in, act_out, grad_out, sem):
    copies = []
    for n, (src, dst) in enumerate(((act_in, act_out), (grad_in, grad_out))):
        size = src.shape[0] // 4
        for i in range(4):
            these = pl.ds(i * size, size)
            copies.append(pltpu.make_async_copy(src.at[these], dst.at[these], sem.at[n, i]))
    for copy in copies:
        copy.start()
    for copy in copies:
        copy.wait()


def solution(mesh):
    def local(tokens, weight, cotangent):
        rows, feats = tokens.shape
        depth, width = weight.shape
        n_row, n_col = mesh.shape["row"], mesh.shape["col"]
        chunks = len(WIDTHS)
        mid = rows // 2
        bf16, f32 = jnp.bfloat16, jnp.float32
        dma = pltpu.SemaphoreType.DMA
        results = pl.pallas_call(
            kernel,
            out_shape=(
                pltpu.VMEM((rows, width), bf16),
                pltpu.VMEM((rows, feats), bf16),
            ),
            in_specs=[pl.BlockSpec(memory_space=pl.ANY)] * 3,
            out_specs=(pl.BlockSpec(memory_space=pltpu.VMEM),) * 2,
            scratch_shapes=[
                pltpu.VMEM((rows, feats * n_col), bf16),
                tuple(pltpu.VMEM((depth * n_row, size), bf16) for size in WIDTHS),
                pltpu.VMEM((rows, width), bf16),
                pltpu.VMEM((rows, width), f32),
                pltpu.VMEM((rows, width), bf16),
                pltpu.VMEM((8, mid, feats), bf16),
                pltpu.VMEM((8, mid, feats), bf16),
                pltpu.VMEM((6, mid, feats), bf16),
                pltpu.VMEM((2, mid, feats), bf16),
                pltpu.VMEM((2, 2, mid, feats), bf16),
                pltpu.VMEM((2 * EARLY, mid, feats), f32),
                pltpu.VMEM((rows, feats), f32),
                pltpu.VMEM((mid, feats), f32),
                dma((3,)),
                dma((chunks,)),
                dma((chunks,)),
                dma((chunks, 2, 20)),
                dma,
                dma((8,)),
                dma((len(STEPS),)),
                dma((len(STEPS),)),
                dma((len(STEPS),)),
                dma((len(STEPS),)),
            ],
            compiler_params=pltpu.CompilerParams(
                collective_id=0, has_side_effects=True, vmem_limit_bytes=52 << 20
            ),
            cost_estimate=pl.CostEstimate(
                flops=4 * rows * feats * n_col * width, bytes_accessed=1 << 24, transcendentals=2 * rows * width
            ),
        )(tokens, weight, cotangent)
        return pl.pallas_call(
            hand_on,
            out_shape=tuple(jax.ShapeDtypeStruct(a.shape, a.dtype) for a in results),
            in_specs=[pl.BlockSpec(memory_space=pltpu.VMEM)] * 2,
            out_specs=(pl.BlockSpec(memory_space=pl.ANY),) * 2,
            scratch_shapes=[dma((2, 4))],
            compiler_params=pltpu.CompilerParams(vmem_limit_bytes=8 << 20),
        )(*results)

    in_specs = (P("row", "col"), P("row", "col"), P("row", "col"))
    out_specs = (P("row", "col"), P("row", "col"))
    return jax.shard_map(local, mesh=mesh, in_specs=in_specs, out_specs=out_specs, check_vma=False)
```

```python
import functools
import math

import jax
import jax.numpy as jnp
from jax import lax
from jax.experimental import pallas as pl
from jax.experimental.pallas import tpu as pltpu
from jax.sharding import PartitionSpec as P

MESH = pl.DeviceIdType.MESH
RING = 4
CORES = 2
WIDTHS = (512, 512, 512)
STARTS = tuple(sum(WIDTHS[:i]) for i in range(len(WIDTHS)))
STEPS = ((2, 0), (2, 1), (1, 1), (3, 0), (1, 0), (3, 1), (0, 0), (0, 1))
EARLY = 2
EARLY_CHUNKS, EARLY_TICK = 1, 3

def gelu_parts(pre):
    cdf = 0.5 * (1.0 + lax.erf(pre * (1.0 / math.sqrt(2.0))))
    pdf = jnp.exp(-0.5 * pre * pre) * (1.0 / math.sqrt(2.0 * math.pi))
    return (pre * cdf, cdf + pre * pdf)


def kernel(
    tok_hbm, w_hbm, cot_hbm, act, grad,
    tok, ws, cot, pre, gp, part_out, part_in, staged, first_in, last_in, begun, own, total,
    load_sem, w_sem, w_send, w_recv, t_send, t_recv, d_send, d_recv, x_send, x_recv,
):
    rows, feats = tok_hbm.shape
    depth, width = w_hbm.shape
    chunks = len(WIDTHS)
    fam = depth // 2
    half = fam // 2
    mid = rows // 2

    r, c = lax.axis_index("row"), lax.axis_index("col")
    y, z = lax.div(r, RING), lax.rem(r, RING)
    x, k = lax.div(c, CORES), lax.rem(c, CORES)

    def at(y, z, x, k):
        return (lax.rem(y, RING) * RING + lax.rem(z, RING), lax.rem(x, RING) * CORES + k)

    neighbours = [
        at(y + 1, z, x, k), at(y + 3, z, x, k), at(y, z + 1, x, k), at(y, z + 3, x, k),
        at(y, z, x + 1, k), at(y, z, x + 3, k), at(y, z, x, 1 - k),
    ]
    x_up, x_down, twin = neighbours[4:]

    def send(src, dst, ssem, rsem, device):
        pltpu.make_async_remote_copy(
            src_ref=src, dst_ref=dst, send_sem=ssem, recv_sem=rsem, device_id=device, device_id_type=MESH
        ).start()

    def arrived(dst, ssem, rsem):
        pltpu.make_async_remote_copy(
            src_ref=dst, dst_ref=dst, send_sem=ssem, recv_sem=rsem, device_id=twin, device_id_type=MESH
        ).wait_recv()

    def sent(src, ssem, rsem):
        pltpu.make_async_remote_copy(
            src_ref=src, dst_ref=src, send_sem=ssem, recv_sem=rsem, device_id=twin, device_id_type=MESH
        ).wait_send()

    def tok_at(x, k, row=0, size=rows):
        return tok.at[pl.ds(row, size), pl.ds(pl.multiple_of((lax.rem(x, RING) * CORES + k) * feats, 128), feats)]

    def w_load(ch):
        return pltpu.make_async_copy(
            w_hbm.at[:, pl.ds(STARTS[ch], WIDTHS[ch])],
            ws[ch].at[pl.ds(pl.multiple_of(r * depth, 16), depth)],
            w_sem.at[ch],
        )

    for ch in range(chunks):
        w_load(ch).start()
    def t_load():
        return pltpu.make_async_copy(tok_hbm, tok_at(x, k), load_sem.at[1])

    def c_load():
        return pltpu.make_async_copy(cot_hbm, cot, load_sem.at[2])

    t_load().start()
    c_load().start()

    barrier = pltpu.get_barrier_semaphore()
    for device in neighbours:
        pl.semaphore_signal(barrier, inc=1, device_id=device, device_id_type=MESH)
    pl.semaphore_wait(barrier, len(neighbours))

    at_block = [
        [pl.multiple_of((lax.rem(y + dy, RING) * RING + lax.rem(z + dz, RING)) * depth, 16) for dz in range(RING)]
        for dy in range(RING)
    ]
    ring_y, ring_z = neighbours[0:2], neighbours[2:4]

    def unit(f, dp, dq, ch, row=0, size=fam):
        dy, dz = (dp, dq) if f == 0 else (dq, dp)
        return ws[ch].at[pl.ds(at_block[dy % RING][dz % RING] + (f * fam + row), size)]

    def parts(f, ch, n):
        way = n % 2
        back = (-1, 1)[way]
        first, second = (ring_y, ring_z) if f == 0 else (ring_z, ring_y)
        cut = (way * half, half)
        if n < 2:
            return unit(f, 0, 0, ch), unit(f, back, 0, ch), first[way]
        if n < 4:
            return unit(f, back, 0, ch, *cut), unit(f, 2, 0, ch, *cut), first[way]
        place = (0, -1, 1, 2)[(n - 4) % 8 // 2]
        if n < 12:
            return unit(f, place, 0, ch), unit(f, place, back, ch), second[way]
        return unit(f, place, back, ch, *cut), unit(f, place, 2, ch, *cut), second[way]

    def push(f, ch, *ns):
        for n in ns:
            out, _, device = parts(f, ch, n)
            send(out, out, w_send.at[ch], w_recv.at[ch, f, n], device)

    def landed(f, ch, *ns):
        for n in ns:
            arrived(parts(f, ch, n)[1], w_send.at[ch], w_recv.at[ch, f, n])

    def stage0(ch):
        w_load(ch).wait()
        for f in range(2):
            push(f, ch, 0, 1)
        for f in range(2):
            push(f, ch, 4, 5)

    def stage1(f, ch):
        for way in range(2):
            landed(f, ch, way)
            push(f, ch, 2 + way, 6 + 2 * way, 7 + 2 * way)
        for way in range(2):
            landed(f, ch, 4 + way)
            push(f, ch, 12 + way)

    def stage2(f, ch):
        landed(f, ch, 2, 3)
        push(f, ch, 10, 11)
        for n in (6, 7, 8, 9):
            landed(f, ch, n)
            push(f, ch, 8 + n)

    def stage3(f, ch):
        for n in (10, 11):
            landed(f, ch, n)
            push(f, ch, 8 + n)

    ends = ((), (), (12, 13), (14, 15, 16, 17), (18, 19))

    blocks = (
        ((0, 0),),
        ((1, 0), (3, 0), (0, 1), (0, 3)),
        ((2, 0), (0, 2), (1, 1), (1, 3), (3, 1), (3, 3)),
        ((1, 2), (3, 2), (2, 1), (2, 3)),
        ((2, 2),),
    )

    def accumulate(ch, stage):
        columns = pl.ds(STARTS[ch], WIDTHS[ch])
        for f in range(2):
            landed(f, ch, *ends[stage])

        for dy, dz in blocks[stage]:
            there = pl.ds(at_block[dy][dz], depth)

            def body(i, _):
                these = pl.ds(pl.multiple_of(i * mid, 16), mid)
                part = jnp.dot(tok[these, there], ws[ch][there, :], preferred_element_type=jnp.float32)
                pre[these, columns] = part if stage == 0 else pre[these, columns] + part
                return 0

            lax.fori_loop(0, 2, body, 0)

    def tokens0():
        send(tok_at(x, k), tok_at(x, k), t_send, t_recv.at[0], x_up)
        send(tok_at(x, k), tok_at(x, k), t_send, t_recv.at[1], x_down)
        send(tok_at(x, k), tok_at(x, k), t_send, t_recv.at[4], twin)

    def tokens1():
        for way, there, device in ((0, x + 3, x_up), (1, x + 1, x_down)):
            arrived(tok_at(there, k), t_send, t_recv.at[way])
            piece = tok_at(there, k, way * mid, mid)
            send(piece, piece, t_send, t_recv.at[2 + way], device)
            send(tok_at(there, k), tok_at(there, k), t_send, t_recv.at[5 + way], twin)

    def tokens2():
        for way in range(2):
            arrived(tok_at(x + 2, k, way * mid, mid), t_send, t_recv.at[2 + way])
        send(tok_at(x + 2, k), tok_at(x + 2, k), t_send, t_recv.at[7], twin)

    def tokens3():
        for j, there in enumerate((x, x + 3, x + 1, x + 2)):
            arrived(tok_at(there, 1 - k), t_send, t_recv.at[4 + j])

    def activate(ch, half_from):
        columns = pl.ds(STARTS[ch], WIDTHS[ch])
        step = rows // 4

        def body(i, _):
            these = pl.ds(pl.multiple_of(i * step, 16), step)
            value, slope = gelu_parts(pre[these, columns])
            act[these, columns] = value.astype(jnp.bfloat16)
            gp[these, columns] = (cot[these, columns].astype(jnp.float32) * slope).astype(jnp.bfloat16)
            return 0

        lax.fori_loop(half_from * 2, half_from * 2 + 2, body, 0)

    def product(s, core, dst, chs, begun=None):
        dx, h = STEPS[s]
        tile = 256 if begun is None else feats

        def body(n, _):
            begin = (lax.rem(x + dx, RING) * CORES + core) * feats + n * tile
            columns = pl.ds(pl.multiple_of(n * tile, 128), tile)
            part = 0.0 if begun is None else begun[:, columns]
            for ch in chs:
                part += lax.dot_general(
                    gp[pl.ds(h * mid, mid), pl.ds(STARTS[ch], WIDTHS[ch])],
                    ws[ch][pl.ds(pl.multiple_of(begin, 128), tile), :],
                    (((1,), (1,)), ((), ())),
                    preferred_element_type=jnp.float32,
                )
            dst[:, columns] = part.astype(dst.dtype)
            return 0

        lax.fori_loop(0, feats // tile, body, 0)

    chs = tuple(range(chunks))
    stages = (None, stage1, stage2, stage3)
    behind = []
    stage0(0)
    t_load().wait()
    tokens0()
    if chunks > 1:
        stage0(1)
    behind += [(ch, 0) for ch in range(chunks)]
    for t in range(1, chunks + 3):
        for lag in (3, 2, 1):
            for f in range(2):
                if 0 <= t - lag < chunks:
                    stages[lag](f, t - lag)
        if t + 1 < chunks:
            stage0(t + 1)
        behind += [(t - lag, lag) for lag in (3, 2, 1) if 0 <= t - lag < chunks]
        if t == 1:
            tokens1()
            tokens2()
        if t == 2:
            tokens3()
            c_load().wait()
        if t >= 2:
            for ch, stage in sorted(behind):
                accumulate(ch, stage)
            behind = []
        if t >= 3:
            accumulate(t - 3, 4)
            if t < chunks + 2:
                activate(t - 3, 0)
                activate(t - 3, 1)
        if t == EARLY_TICK:
            for n in range(2 * EARLY):
                product(n // 2, (1 - k, k)[n % 2], begun.at[n], chs[:EARLY_CHUNKS])

    sent(tok.at[:, pl.ds(0, (2 * RING - 1) * feats)], t_send, t_send)

    def finish(s, n, core, dst):
        if s < EARLY:
            product(s, core, dst, chs[EARLY_CHUNKS:], begun.at[2 * s + n])
        else:
            product(s, core, dst, chs)

    def for_twin(s):
        finish(s, 0, 1 - k, part_out.at[s])
        send(part_out.at[s], part_in.at[s], d_send.at[s], d_recv.at[s], twin)

    def pieces(s):
        dx, h = STEPS[s]
        if dx != 2 and h == dx // 2:
            return [(pl.ds(i * (mid // 2), mid // 2), s + 2 * i) for i in range(2)]
        return [(pl.ds(0, mid), s)]

    for s in range(EARLY):
        activate(chunks - 1, s)
        for_twin(s)
    for s, (dx, h) in enumerate(STEPS):
        for later in range(EARLY, 4) if s == 2 else (s + 1,) if s > 2 else ():
            if later < len(STEPS):
                for_twin(later)
        mine = own.at[pl.ds(h * mid, mid)] if dx == 0 else total
        finish(s, 1, k, mine)
        arrived(part_in.at[s], d_send.at[s], d_recv.at[s])
        summed = mine[...] + part_in[s].astype(jnp.float32)
        if dx == 0:
            mine[...] = summed
            continue
        way = h if dx == 2 else dx // 2
        if dx != 2 and h == way:
            arrived(first_in.at[way], x_send.at[way], x_recv.at[way])
            summed = summed + first_in[way].astype(jnp.float32)
        staged[s] = summed.astype(jnp.bfloat16)
        for piece, sem in pieces(s):
            into = first_in.at[h] if dx == 2 else last_in.at[way, h, piece]
            send(staged.at[s, piece], into, x_send.at[sem], x_recv.at[sem], (x_up, x_down)[way])

    for i in range(2):
        for h in range(2):
            for way, dx in enumerate((1, 3)):
                these = pieces(STEPS.index((dx, h)))
                if i < len(these):
                    piece, sem = these[i]
                    arrived(last_in.at[way, h, piece], x_send.at[sem], x_recv.at[sem])
            size = mid // 2
            these, inner = pl.ds(h * mid + i * size, size), pl.ds(i * size, size)
            result = own[these, :] + last_in[0, h, inner].astype(jnp.float32) + last_in[1, h, inner].astype(jnp.float32)
            grad[these, :] = result.astype(jnp.bfloat16)

    for s, (dx, _) in enumerate(STEPS):
        sent(part_out.at[s], d_send.at[s], d_recv.at[s])
        if dx:
            for piece, sem in pieces(s):
                sent(staged.at[s, piece], x_send.at[sem], x_recv.at[sem])
    ring = RING * RING - 1
    for ch in range(chunks):
        sent(ws[ch].at[pl.ds(0, ring * depth)], w_send.at[ch], w_send.at[ch])


def hand_on(act_in, grad_in, act_out, grad_out, sem):
    copies = []
    for n, (src, dst) in enumerate(((act_in, act_out), (grad_in, grad_out))):
        size = src.shape[0] // 4
        for i in range(4):
            these = pl.ds(i * size, size)
            copies.append(pltpu.make_async_copy(src.at[these], dst.at[these], sem.at[n, i]))
    for copy in copies:
        copy.start()
    for copy in copies:
        copy.wait()


def solution(mesh):
    def local(tokens, weight, cotangent):
        rows, feats = tokens.shape
        depth, width = weight.shape
        n_row, n_col = mesh.shape["row"], mesh.shape["col"]
        chunks = len(WIDTHS)
        mid = rows // 2
        bf16, f32 = jnp.bfloat16, jnp.float32
        dma = pltpu.SemaphoreType.DMA
        results = pl.pallas_call(
            kernel,
            out_shape=(
                pltpu.VMEM((rows, width), bf16),
                pltpu.VMEM((rows, feats), bf16),
            ),
            in_specs=[pl.BlockSpec(memory_space=pl.ANY)] * 3,
            out_specs=(pl.BlockSpec(memory_space=pltpu.VMEM),) * 2,
            scratch_shapes=[
                pltpu.VMEM((rows, feats * n_col), bf16),
                tuple(pltpu.VMEM((depth * n_row, size), bf16) for size in WIDTHS),
                pltpu.VMEM((rows, width), bf16),
                pltpu.VMEM((rows, width), f32),
                pltpu.VMEM((rows, width), bf16),
                pltpu.VMEM((8, mid, feats), bf16),
                pltpu.VMEM((8, mid, feats), bf16),
                pltpu.VMEM((6, mid, feats), bf16),
                pltpu.VMEM((2, mid, feats), bf16),
                pltpu.VMEM((2, 2, mid, feats), bf16),
                pltpu.VMEM((2 * EARLY, mid, feats), f32),
                pltpu.VMEM((rows, feats), f32),
                pltpu.VMEM((mid, feats), f32),
                dma((3,)),
                dma((chunks,)),
                dma((chunks,)),
                dma((chunks, 2, 20)),
                dma,
                dma((8,)),
                dma((len(STEPS),)),
                dma((len(STEPS),)),
                dma((len(STEPS),)),
                dma((len(STEPS),)),
            ],
            compiler_params=pltpu.CompilerParams(
                collective_id=0, has_side_effects=True, vmem_limit_bytes=52 << 20
            ),
            cost_estimate=pl.CostEstimate(
                flops=4 * rows * feats * n_col * width, bytes_accessed=1 << 24, transcendentals=2 * rows * width
            ),
        )(tokens, weight, cotangent)
        return pl.pallas_call(
            hand_on,
            out_shape=tuple(jax.ShapeDtypeStruct(a.shape, a.dtype) for a in results),
            in_specs=[pl.BlockSpec(memory_space=pltpu.VMEM)] * 2,
            out_specs=(pl.BlockSpec(memory_space=pl.ANY),) * 2,
            scratch_shapes=[dma((2, 4))],
            compiler_params=pltpu.CompilerParams(vmem_limit_bytes=8 << 20),
        )(*results)

    in_specs = (P("row", "col"), P("row", "col"), P("row", "col"))
    out_specs = (P("row", "col"), P("row", "col"))
    return jax.shard_map(local, mesh=mesh, in_specs=in_specs, out_specs=out_specs, check_vma=False)
```

```python
import functools
import math

import jax
import jax.numpy as jnp
from jax import lax
from jax.experimental import pallas as pl
from jax.experimental.pallas import tpu as pltpu
from jax.sharding import PartitionSpec as P

MESH = pl.DeviceIdType.MESH
RING = 4
CORES = 2
WIDTHS = (512, 512, 512)
STARTS = tuple(sum(WIDTHS[:i]) for i in range(len(WIDTHS)))
STEPS = ((2, 0), (2, 1), (1, 1), (3, 0), (1, 0), (3, 1), (0, 0), (0, 1))
EARLY = 2
EARLY_CHUNKS, EARLY_TICK = 1, 3

def gelu_parts(pre):
    cdf = 0.5 * (1.0 + lax.erf(pre * (1.0 / math.sqrt(2.0))))
    pdf = jnp.exp(-0.5 * pre * pre) * (1.0 / math.sqrt(2.0 * math.pi))
    return (pre * cdf, cdf + pre * pdf)


def kernel(
    tok_hbm, w_hbm, cot_hbm, act, grad,
    tok, ws, cot, pre, gp, part_out, part_in, staged, first_in, last_in, begun, own, total,
    load_sem, w_sem, w_send, w_recv, t_send, t_recv, d_send, d_recv, x_send, x_recv,
):
    rows, feats = tok_hbm.shape
    depth, width = w_hbm.shape
    chunks = len(WIDTHS)
    fam = depth // 2
    half = fam // 2
    mid = rows // 2

    r, c = lax.axis_index("row"), lax.axis_index("col")
    y, z = lax.div(r, RING), lax.rem(r, RING)
    x, k = lax.div(c, CORES), lax.rem(c, CORES)

    def at(y, z, x, k):
        return (lax.rem(y, RING) * RING + lax.rem(z, RING), lax.rem(x, RING) * CORES + k)

    neighbours = [
        at(y + 1, z, x, k), at(y + 3, z, x, k), at(y, z + 1, x, k), at(y, z + 3, x, k),
        at(y, z, x + 1, k), at(y, z, x + 3, k), at(y, z, x, 1 - k),
    ]
    x_up, x_down, twin = neighbours[4:]

    def send(src, dst, ssem, rsem, device):
        pltpu.make_async_remote_copy(
            src_ref=src, dst_ref=dst, send_sem=ssem, recv_sem=rsem, device_id=device, device_id_type=MESH
        ).start()

    def arrived(dst, ssem, rsem):
        pltpu.make_async_remote_copy(
            src_ref=dst, dst_ref=dst, send_sem=ssem, recv_sem=rsem, device_id=twin, device_id_type=MESH
        ).wait_recv()

    def sent(src, ssem, rsem):
        pltpu.make_async_remote_copy(
            src_ref=src, dst_ref=src, send_sem=ssem, recv_sem=rsem, device_id=twin, device_id_type=MESH
        ).wait_send()

    def tok_at(x, k, row=0, size=rows):
        return tok.at[pl.ds(row, size), pl.ds(pl.multiple_of((lax.rem(x, RING) * CORES + k) * feats, 128), feats)]

    def w_load(ch):
        return pltpu.make_async_copy(
            w_hbm.at[:, pl.ds(STARTS[ch], WIDTHS[ch])],
            ws[ch].at[pl.ds(pl.multiple_of(r * depth, 16), depth)],
            w_sem.at[ch],
        )

    for ch in range(chunks):
        w_load(ch).start()
    def t_load():
        return pltpu.make_async_copy(tok_hbm, tok_at(x, k), load_sem.at[1])

    def c_load():
        return pltpu.make_async_copy(cot_hbm, cot, load_sem.at[2])

    t_load().start()
    c_load().start()

    barrier = pltpu.get_barrier_semaphore()
    for device in neighbours:
        pl.semaphore_signal(barrier, inc=1, device_id=device, device_id_type=MESH)
    pl.semaphore_wait(barrier, len(neighbours))

    at_block = [
        [pl.multiple_of((lax.rem(y + dy, RING) * RING + lax.rem(z + dz, RING)) * depth, 16) for dz in range(RING)]
        for dy in range(RING)
    ]
    ring_y, ring_z = neighbours[0:2], neighbours[2:4]

    def unit(f, dp, dq, ch, row=0, size=fam):
        dy, dz = (dp, dq) if f == 0 else (dq, dp)
        return ws[ch].at[pl.ds(at_block[dy % RING][dz % RING] + (f * fam + row), size)]

    def parts(f, ch, n):
        way = n % 2
        back = (-1, 1)[way]
        first, second = (ring_y, ring_z) if f == 0 else (ring_z, ring_y)
        cut = (way * half, half)
        if n < 2:
            return unit(f, 0, 0, ch), unit(f, back, 0, ch), first[way]
        if n < 4:
            return unit(f, back, 0, ch, *cut), unit(f, 2, 0, ch, *cut), first[way]
        place = (0, -1, 1, 2)[(n - 4) % 8 // 2]
        if n < 12:
            return unit(f, place, 0, ch), unit(f, place, back, ch), second[way]
        return unit(f, place, back, ch, *cut), unit(f, place, 2, ch, *cut), second[way]

    def push(f, ch, *ns):
        for n in ns:
            out, _, device = parts(f, ch, n)
            send(out, out, w_send.at[ch], w_recv.at[ch, f, n], device)

    def landed(f, ch, *ns):
        for n in ns:
            arrived(parts(f, ch, n)[1], w_send.at[ch], w_recv.at[ch, f, n])

    def stage0(ch):
        w_load(ch).wait()
        for f in range(2):
            push(f, ch, 0, 1)
        for f in range(2):
            push(f, ch, 4, 5)

    def stage1(f, ch):
        for way in range(2):
            landed(f, ch, way)
            push(f, ch, 2 + way, 6 + 2 * way, 7 + 2 * way)
        for way in range(2):
            landed(f, ch, 4 + way)
            push(f, ch, 12 + way)

    def stage2(f, ch):
        landed(f, ch, 2, 3)
        push(f, ch, 10, 11)
        for n in (6, 7, 8, 9):
            landed(f, ch, n)
            push(f, ch, 8 + n)

    def stage3(f, ch):
        for n in (10, 11):
            landed(f, ch, n)
            push(f, ch, 8 + n)

    ends = ((), (), (12, 13), (14, 15, 16, 17), (18, 19))

    blocks = (
        ((0, 0),),
        ((1, 0), (3, 0), (0, 1), (0, 3)),
        ((2, 0), (0, 2), (1, 1), (1, 3), (3, 1), (3, 3)),
        ((1, 2), (3, 2), (2, 1), (2, 3)),
        ((2, 2),),
    )

    def accumulate(ch, stage):
        columns = pl.ds(STARTS[ch], WIDTHS[ch])
        for f in range(2):
            landed(f, ch, *ends[stage])

        for dy, dz in blocks[stage]:
            there = pl.ds(at_block[dy][dz], depth)

            def body(i, _):
                these = pl.ds(pl.multiple_of(i * mid, 16), mid)
                part = jnp.dot(tok[these, there], ws[ch][there, :], preferred_element_type=jnp.float32)
                pre[these, columns] = part if stage == 0 else pre[these, columns] + part
                return 0

            lax.fori_loop(0, 2, body, 0)

    def tokens0():
        send(tok_at(x, k), tok_at(x, k), t_send, t_recv.at[0], x_up)
        send(tok_at(x, k), tok_at(x, k), t_send, t_recv.at[1], x_down)
        send(tok_at(x, k), tok_at(x, k), t_send, t_recv.at[4], twin)

    def tokens1():
        for way, there, device in ((0, x + 3, x_up), (1, x + 1, x_down)):
            arrived(tok_at(there, k), t_send, t_recv.at[way])
            piece = tok_at(there, k, way * mid, mid)
            send(piece, piece, t_send, t_recv.at[2 + way], device)
            send(tok_at(there, k), tok_at(there, k), t_send, t_recv.at[5 + way], twin)

    def tokens2():
        for way in range(2):
            arrived(tok_at(x + 2, k, way * mid, mid), t_send, t_recv.at[2 + way])
        send(tok_at(x + 2, k), tok_at(x + 2, k), t_send, t_recv.at[7], twin)

    def tokens3():
        for j, there in enumerate((x, x + 3, x + 1, x + 2)):
            arrived(tok_at(there, 1 - k), t_send, t_recv.at[4 + j])

    def activate(ch, half_from):
        columns = pl.ds(STARTS[ch], WIDTHS[ch])
        step = rows // 4

        def body(i, _):
            these = pl.ds(pl.multiple_of(i * step, 16), step)
            value, slope = gelu_parts(pre[these, columns])
            act[these, columns] = value.astype(jnp.bfloat16)
            gp[these, columns] = (cot[these, columns].astype(jnp.float32) * slope).astype(jnp.bfloat16)
            return 0

        lax.fori_loop(half_from * 2, half_from * 2 + 2, body, 0)

    def product(s, core, dst, chs, begun=None):
        dx, h = STEPS[s]
        tile = 256 if begun is None else feats

        def body(n, _):
            begin = (lax.rem(x + dx, RING) * CORES + core) * feats + n * tile
            columns = pl.ds(pl.multiple_of(n * tile, 128), tile)
            part = 0.0 if begun is None else begun[:, columns]
            for ch in chs:
                part += lax.dot_general(
                    gp[pl.ds(h * mid, mid), pl.ds(STARTS[ch], WIDTHS[ch])],
                    ws[ch][pl.ds(pl.multiple_of(begin, 128), tile), :],
                    (((1,), (1,)), ((), ())),
                    preferred_element_type=jnp.float32,
                )
            dst[:, columns] = part.astype(dst.dtype)
            return 0

        lax.fori_loop(0, feats // tile, body, 0)

    chs = tuple(range(chunks))
    stages = (None, stage1, stage2, stage3)
    behind = []
    stage0(0)
    t_load().wait()
    tokens0()
    if chunks > 1:
        stage0(1)
    behind += [(ch, 0) for ch in range(chunks)]
    for t in range(1, chunks + 3):
        for lag in (3, 2, 1):
            for f in range(2):
                if 0 <= t - lag < chunks:
                    stages[lag](f, t - lag)
        if t + 1 < chunks:
            stage0(t + 1)
        behind += [(t - lag, lag) for lag in (3, 2, 1) if 0 <= t - lag < chunks]
        if t == 1:
            tokens1()
            tokens2()
        if t == 2:
            tokens3()
            c_load().wait()
        if t >= 2:
            for ch, stage in sorted(behind):
                accumulate(ch, stage)
            behind = []
        if t >= 3:
            accumulate(t - 3, 4)
            if t < chunks + 2:
                activate(t - 3, 0)
                activate(t - 3, 1)
        if t == EARLY_TICK:
            for n in range(2 * EARLY):
                product(n // 2, (1 - k, k)[n % 2], begun.at[n], chs[:EARLY_CHUNKS])
        if t == chunks + 1:
            for n in range(2 * EARLY):
                product(n // 2, (1 - k, k)[n % 2], begun.at[n], chs[EARLY_CHUNKS:-1], begun.at[n])

    sent(tok.at[:, pl.ds(0, (2 * RING - 1) * feats)], t_send, t_send)

    def finish(s, n, core, dst):
        if s < EARLY:
            product(s, core, dst, chs[-1:], begun.at[2 * s + n])
        else:
            product(s, core, dst, chs)

    def for_twin(s):
        finish(s, 0, 1 - k, part_out.at[s])
        send(part_out.at[s], part_in.at[s], d_send.at[s], d_recv.at[s], twin)

    def pieces(s):
        dx, h = STEPS[s]
        if dx != 2 and h == dx // 2:
            return [(pl.ds(i * (mid // 2), mid // 2), s + 2 * i) for i in range(2)]
        return [(pl.ds(0, mid), s)]

    for s in range(EARLY):
        activate(chunks - 1, s)
        for_twin(s)
    for s, (dx, h) in enumerate(STEPS):
        for later in range(EARLY, 4) if s == 2 else (s + 1,) if s > 2 else ():
            if later < len(STEPS):
                for_twin(later)
        mine = own.at[pl.ds(h * mid, mid)] if dx == 0 else total
        finish(s, 1, k, mine)
        arrived(part_in.at[s], d_send.at[s], d_recv.at[s])
        summed = mine[...] + part_in[s].astype(jnp.float32)
        if dx == 0:
            mine[...] = summed
            continue
        way = h if dx == 2 else dx // 2
        if dx != 2 and h == way:
            arrived(first_in.at[way], x_send.at[way], x_recv.at[way])
            summed = summed + first_in[way].astype(jnp.float32)
        staged[s] = summed.astype(jnp.bfloat16)
        for piece, sem in pieces(s):
            into = first_in.at[h] if dx == 2 else last_in.at[way, h, piece]
            send(staged.at[s, piece], into, x_send.at[sem], x_recv.at[sem], (x_up, x_down)[way])

    for i in range(2):
        for h in range(2):
            for way, dx in enumerate((1, 3)):
                these = pieces(STEPS.index((dx, h)))
                if i < len(these):
                    piece, sem = these[i]
                    arrived(last_in.at[way, h, piece], x_send.at[sem], x_recv.at[sem])
            size = mid // 2
            these, inner = pl.ds(h * mid + i * size, size), pl.ds(i * size, size)
            result = own[these, :] + last_in[0, h, inner].astype(jnp.float32) + last_in[1, h, inner].astype(jnp.float32)
            grad[these, :] = result.astype(jnp.bfloat16)

    for s, (dx, _) in enumerate(STEPS):
        sent(part_out.at[s], d_send.at[s], d_recv.at[s])
        if dx:
            for piece, sem in pieces(s):
                sent(staged.at[s, piece], x_send.at[sem], x_recv.at[sem])
    ring = RING * RING - 1
    for ch in range(chunks):
        sent(ws[ch].at[pl.ds(0, ring * depth)], w_send.at[ch], w_send.at[ch])


def hand_on(act_in, grad_in, act_out, grad_out, sem):
    copies = []
    for n, (src, dst) in enumerate(((act_in, act_out), (grad_in, grad_out))):
        size = src.shape[0] // 4
        for i in range(4):
            these = pl.ds(i * size, size)
            copies.append(pltpu.make_async_copy(src.at[these], dst.at[these], sem.at[n, i]))
    for copy in copies:
        copy.start()
    for copy in copies:
        copy.wait()


def solution(mesh):
    def local(tokens, weight, cotangent):
        rows, feats = tokens.shape
        depth, width = weight.shape
        n_row, n_col = mesh.shape["row"], mesh.shape["col"]
        chunks = len(WIDTHS)
        mid = rows // 2
        bf16, f32 = jnp.bfloat16, jnp.float32
        dma = pltpu.SemaphoreType.DMA
        results = pl.pallas_call(
            kernel,
            out_shape=(
                pltpu.VMEM((rows, width), bf16),
                pltpu.VMEM((rows, feats), bf16),
            ),
            in_specs=[pl.BlockSpec(memory_space=pl.ANY)] * 3,
            out_specs=(pl.BlockSpec(memory_space=pltpu.VMEM),) * 2,
            scratch_shapes=[
                pltpu.VMEM((rows, feats * n_col), bf16),
                tuple(pltpu.VMEM((depth * n_row, size), bf16) for size in WIDTHS),
                pltpu.VMEM((rows, width), bf16),
                pltpu.VMEM((rows, width), f32),
                pltpu.VMEM((rows, width), bf16),
                pltpu.VMEM((8, mid, feats), bf16),
                pltpu.VMEM((8, mid, feats), bf16),
                pltpu.VMEM((6, mid, feats), bf16),
                pltpu.VMEM((2, mid, feats), bf16),
                pltpu.VMEM((2, 2, mid, feats), bf16),
                pltpu.VMEM((2 * EARLY, mid, feats), f32),
                pltpu.VMEM((rows, feats), f32),
                pltpu.VMEM((mid, feats), f32),
                dma((3,)),
                dma((chunks,)),
                dma((chunks,)),
                dma((chunks, 2, 20)),
                dma,
                dma((8,)),
                dma((len(STEPS),)),
                dma((len(STEPS),)),
                dma((len(STEPS),)),
                dma((len(STEPS),)),
            ],
            compiler_params=pltpu.CompilerParams(
                collective_id=0, has_side_effects=True, vmem_limit_bytes=52 << 20
            ),
            cost_estimate=pl.CostEstimate(
                flops=4 * rows * feats * n_col * width, bytes_accessed=1 << 24, transcendentals=2 * rows * width
            ),
        )(tokens, weight, cotangent)
        return pl.pallas_call(
            hand_on,
            out_shape=tuple(jax.ShapeDtypeStruct(a.shape, a.dtype) for a in results),
            in_specs=[pl.BlockSpec(memory_space=pltpu.VMEM)] * 2,
            out_specs=(pl.BlockSpec(memory_space=pl.ANY),) * 2,
            scratch_shapes=[dma((2, 4))],
            compiler_params=pltpu.CompilerParams(vmem_limit_bytes=8 << 20),
        )(*results)

    in_specs = (P("row", "col"), P("row", "col"), P("row", "col"))
    out_specs = (P("row", "col"), P("row", "col"))
    return jax.shard_map(local, mesh=mesh, in_specs=in_specs, out_specs=out_specs, check_vma=False)
```

```python
import functools
import math

import jax
import jax.numpy as jnp
from jax import lax
from jax.experimental import pallas as pl
from jax.experimental.pallas import tpu as pltpu
from jax.sharding import PartitionSpec as P

MESH = pl.DeviceIdType.MESH
RING = 4
CORES = 2
WIDTHS = (512, 512, 512)
STARTS = tuple(sum(WIDTHS[:i]) for i in range(len(WIDTHS)))
STEPS = ((2, 0), (2, 1), (1, 1), (3, 0), (1, 0), (3, 1), (0, 0), (0, 1))
EARLY = 2
EARLY_CHUNKS, EARLY_TICK = 1, 3

def gelu_parts(pre):
    cdf = 0.5 * (1.0 + lax.erf(pre * (1.0 / math.sqrt(2.0))))
    pdf = jnp.exp(-0.5 * pre * pre) * (1.0 / math.sqrt(2.0 * math.pi))
    return (pre * cdf, cdf + pre * pdf)


def kernel(
    tok_hbm, w_hbm, cot_hbm, act, grad,
    tok, ws, cot, pre, gp, part_out, part_in, staged, first_in, last_in, begun, own, total,
    load_sem, w_sem, w_send, w_recv, t_send, t_recv, d_send, d_recv, x_send, x_recv,
):
    rows, feats = tok_hbm.shape
    depth, width = w_hbm.shape
    chunks = len(WIDTHS)
    fam = depth // 2
    half = fam // 2
    mid = rows // 2

    r, c = lax.axis_index("row"), lax.axis_index("col")
    y, z = lax.div(r, RING), lax.rem(r, RING)
    x, k = lax.div(c, CORES), lax.rem(c, CORES)

    def at(y, z, x, k):
        return (lax.rem(y, RING) * RING + lax.rem(z, RING), lax.rem(x, RING) * CORES + k)

    neighbours = [
        at(y + 1, z, x, k), at(y + 3, z, x, k), at(y, z + 1, x, k), at(y, z + 3, x, k),
        at(y, z, x + 1, k), at(y, z, x + 3, k), at(y, z, x, 1 - k),
    ]
    x_up, x_down, twin = neighbours[4:]

    def send(src, dst, ssem, rsem, device):
        pltpu.make_async_remote_copy(
            src_ref=src, dst_ref=dst, send_sem=ssem, recv_sem=rsem, device_id=device, device_id_type=MESH
        ).start()

    def arrived(dst, ssem, rsem):
        pltpu.make_async_remote_copy(
            src_ref=dst, dst_ref=dst, send_sem=ssem, recv_sem=rsem, device_id=twin, device_id_type=MESH
        ).wait_recv()

    def sent(src, ssem, rsem):
        pltpu.make_async_remote_copy(
            src_ref=src, dst_ref=src, send_sem=ssem, recv_sem=rsem, device_id=twin, device_id_type=MESH
        ).wait_send()

    def tok_at(x, k, row=0, size=rows):
        return tok.at[pl.ds(row, size), pl.ds(pl.multiple_of((lax.rem(x, RING) * CORES + k) * feats, 128), feats)]

    def w_load(ch):
        return pltpu.make_async_copy(
            w_hbm.at[:, pl.ds(STARTS[ch], WIDTHS[ch])],
            ws[ch].at[pl.ds(pl.multiple_of(r * depth, 16), depth)],
            w_sem.at[ch],
        )

    for ch in range(chunks):
        w_load(ch).start()
    def t_load():
        return pltpu.make_async_copy(tok_hbm, tok_at(x, k), load_sem.at[1])

    def c_load():
        return pltpu.make_async_copy(cot_hbm, cot, load_sem.at[2])

    t_load().start()
    c_load().start()

    barrier = pltpu.get_barrier_semaphore()
    for device in neighbours:
        pl.semaphore_signal(barrier, inc=1, device_id=device, device_id_type=MESH)
    pl.semaphore_wait(barrier, len(neighbours))

    at_block = [
        [pl.multiple_of((lax.rem(y + dy, RING) * RING + lax.rem(z + dz, RING)) * depth, 16) for dz in range(RING)]
        for dy in range(RING)
    ]
    ring_y, ring_z = neighbours[0:2], neighbours[2:4]

    def unit(f, dp, dq, ch, row=0, size=fam):
        dy, dz = (dp, dq) if f == 0 else (dq, dp)
        return ws[ch].at[pl.ds(at_block[dy % RING][dz % RING] + (f * fam + row), size)]

    def parts(f, ch, n):
        way = n % 2
        back = (-1, 1)[way]
        first, second = (ring_y, ring_z) if f == 0 else (ring_z, ring_y)
        cut = (way * half, half)
        if n < 2:
            return unit(f, 0, 0, ch), unit(f, back, 0, ch), first[way]
        if n < 4:
            return unit(f, back, 0, ch, *cut), unit(f, 2, 0, ch, *cut), first[way]
        place = (0, -1, 1, 2)[(n - 4) % 8 // 2]
        if n < 12:
            return unit(f, place, 0, ch), unit(f, place, back, ch), second[way]
        return unit(f, place, back, ch, *cut), unit(f, place, 2, ch, *cut), second[way]

    def push(f, ch, *ns):
        for n in ns:
            out, _, device = parts(f, ch, n)
            send(out, out, w_send.at[ch], w_recv.at[ch, f, n], device)

    def landed(f, ch, *ns):
        for n in ns:
            arrived(parts(f, ch, n)[1], w_send.at[ch], w_recv.at[ch, f, n])

    def stage0(ch):
        w_load(ch).wait()
        for f in range(2):
            push(f, ch, 0, 1)
        for f in range(2):
            push(f, ch, 4, 5)

    def stage1(f, ch):
        for way in range(2):
            landed(f, ch, way)
            push(f, ch, 2 + way, 6 + 2 * way, 7 + 2 * way)
        for way in range(2):
            landed(f, ch, 4 + way)
            push(f, ch, 12 + way)

    def stage2(f, ch):
        landed(f, ch, 2, 3)
        push(f, ch, 10, 11)
        for n in (6, 7, 8, 9):
            landed(f, ch, n)
            push(f, ch, 8 + n)

    def stage3(f, ch):
        for n in (10, 11):
            landed(f, ch, n)
            push(f, ch, 8 + n)

    ends = ((), (), (12, 13), (14, 15, 16, 17), (18, 19))

    blocks = (
        ((0, 0),),
        ((1, 0), (3, 0), (0, 1), (0, 3)),
        ((2, 0), (0, 2), (1, 1), (1, 3), (3, 1), (3, 3)),
        ((1, 2), (3, 2), (2, 1), (2, 3)),
        ((2, 2),),
    )

    def accumulate(ch, stage, begin=0, end=2):
        columns = pl.ds(STARTS[ch], WIDTHS[ch])
        for f in range(2):
            if begin == 0:
                landed(f, ch, *ends[stage])

        for dy, dz in blocks[stage]:
            there = pl.ds(at_block[dy][dz], depth)

            def body(i, _):
                these = pl.ds(pl.multiple_of(i * mid, 16), mid)
                part = jnp.dot(tok[these, there], ws[ch][there, :], preferred_element_type=jnp.float32)
                pre[these, columns] = part if stage == 0 else pre[these, columns] + part
                return 0

            lax.fori_loop(begin, end, body, 0)

    def tokens0():
        send(tok_at(x, k), tok_at(x, k), t_send, t_recv.at[0], x_up)
        send(tok_at(x, k), tok_at(x, k), t_send, t_recv.at[1], x_down)
        send(tok_at(x, k), tok_at(x, k), t_send, t_recv.at[4], twin)

    def tokens1():
        for way, there, device in ((0, x + 3, x_up), (1, x + 1, x_down)):
            arrived(tok_at(there, k), t_send, t_recv.at[way])
            piece = tok_at(there, k, way * mid, mid)
            send(piece, piece, t_send, t_recv.at[2 + way], device)
            send(tok_at(there, k), tok_at(there, k), t_send, t_recv.at[5 + way], twin)

    def tokens2():
        for way in range(2):
            arrived(tok_at(x + 2, k, way * mid, mid), t_send, t_recv.at[2 + way])
        send(tok_at(x + 2, k), tok_at(x + 2, k), t_send, t_recv.at[7], twin)

    def tokens3():
        for j, there in enumerate((x, x + 3, x + 1, x + 2)):
            arrived(tok_at(there, 1 - k), t_send, t_recv.at[4 + j])

    def activate(ch, half_from):
        columns = pl.ds(STARTS[ch], WIDTHS[ch])
        step = rows // 4

        def body(i, _):
            these = pl.ds(pl.multiple_of(i * step, 16), step)
            value, slope = gelu_parts(pre[these, columns])
            act[these, columns] = value.astype(jnp.bfloat16)
            gp[these, columns] = (cot[these, columns].astype(jnp.float32) * slope).astype(jnp.bfloat16)
            return 0

        lax.fori_loop(half_from * 2, half_from * 2 + 2, body, 0)

    def product(s, core, dst, chs, begun=None):
        dx, h = STEPS[s]
        tile = 256 if begun is None else feats

        def body(n, _):
            begin = (lax.rem(x + dx, RING) * CORES + core) * feats + n * tile
            columns = pl.ds(pl.multiple_of(n * tile, 128), tile)
            part = 0.0 if begun is None else begun[:, columns]
            for ch in chs:
                part += lax.dot_general(
                    gp[pl.ds(h * mid, mid), pl.ds(STARTS[ch], WIDTHS[ch])],
                    ws[ch][pl.ds(pl.multiple_of(begin, 128), tile), :],
                    (((1,), (1,)), ((), ())),
                    preferred_element_type=jnp.float32,
                )
            dst[:, columns] = part.astype(dst.dtype)
            return 0

        lax.fori_loop(0, feats // tile, body, 0)

    chs = tuple(range(chunks))
    stages = (None, stage1, stage2, stage3)
    behind = []
    stage0(0)
    t_load().wait()
    tokens0()
    if chunks > 1:
        stage0(1)
    behind += [(ch, 0) for ch in range(chunks)]
    for t in range(1, chunks + 3):
        for lag in (3, 2, 1):
            for f in range(2):
                if 0 <= t - lag < chunks:
                    stages[lag](f, t - lag)
        if t + 1 < chunks:
            stage0(t + 1)
        behind += [(t - lag, lag) for lag in (3, 2, 1) if 0 <= t - lag < chunks]
        if t == 1:
            tokens1()
            tokens2()
        if t == 2:
            tokens3()
            c_load().wait()
        if t >= 2:
            for ch, stage in sorted(behind):
                accumulate(ch, stage)
            behind = []
        if t >= 3:
            accumulate(t - 3, 4, 0, 1 if t == chunks + 2 else 2)
            if t < chunks + 2:
                activate(t - 3, 0)
                activate(t - 3, 1)
        if t == EARLY_TICK:
            for n in range(2 * EARLY):
                product(n // 2, (1 - k, k)[n % 2], begun.at[n], chs[:EARLY_CHUNKS])
        if t == chunks + 1:
            for n in range(2 * EARLY):
                product(n // 2, (1 - k, k)[n % 2], begun.at[n], chs[EARLY_CHUNKS:-1], begun.at[n])

    sent(tok.at[:, pl.ds(0, (2 * RING - 1) * feats)], t_send, t_send)

    def finish(s, n, core, dst):
        if s < EARLY:
            product(s, core, dst, chs[-1:], begun.at[2 * s + n])
        else:
            product(s, core, dst, chs)

    def for_twin(s):
        finish(s, 0, 1 - k, part_out.at[s])
        send(part_out.at[s], part_in.at[s], d_send.at[s], d_recv.at[s], twin)

    def pieces(s):
        dx, h = STEPS[s]
        if dx != 2 and h == dx // 2:
            return [(pl.ds(i * (mid // 2), mid // 2), s + 2 * i) for i in range(2)]
        return [(pl.ds(0, mid), s)]

    for s in range(EARLY):
        if s == 1:
            accumulate(chunks - 1, 4, 1, 2)
        activate(chunks - 1, s)
        for_twin(s)
    for s, (dx, h) in enumerate(STEPS):
        for later in range(EARLY, 4) if s == 2 else (s + 1,) if s > 2 else ():
            if later < len(STEPS):
                for_twin(later)
        mine = own.at[pl.ds(h * mid, mid)] if dx == 0 else total
        finish(s, 1, k, mine)
        arrived(part_in.at[s], d_send.at[s], d_recv.at[s])
        summed = mine[...] + part_in[s].astype(jnp.float32)
        if dx == 0:
            mine[...] = summed
            continue
        way = h if dx == 2 else dx // 2
        if dx != 2 and h == way:
            arrived(first_in.at[way], x_send.at[way], x_recv.at[way])
            summed = summed + first_in[way].astype(jnp.float32)
        staged[s] = summed.astype(jnp.bfloat16)
        for piece, sem in pieces(s):
            into = first_in.at[h] if dx == 2 else last_in.at[way, h, piece]
            send(staged.at[s, piece], into, x_send.at[sem], x_recv.at[sem], (x_up, x_down)[way])

    for i in range(2):
        for h in range(2):
            for way, dx in enumerate((1, 3)):
                these = pieces(STEPS.index((dx, h)))
                if i < len(these):
                    piece, sem = these[i]
                    arrived(last_in.at[way, h, piece], x_send.at[sem], x_recv.at[sem])
            size = mid // 2
            these, inner = pl.ds(h * mid + i * size, size), pl.ds(i * size, size)
            result = own[these, :] + last_in[0, h, inner].astype(jnp.float32) + last_in[1, h, inner].astype(jnp.float32)
            grad[these, :] = result.astype(jnp.bfloat16)

    for s, (dx, _) in enumerate(STEPS):
        sent(part_out.at[s], d_send.at[s], d_recv.at[s])
        if dx:
            for piece, sem in pieces(s):
                sent(staged.at[s, piece], x_send.at[sem], x_recv.at[sem])
    ring = RING * RING - 1
    for ch in range(chunks):
        sent(ws[ch].at[pl.ds(0, ring * depth)], w_send.at[ch], w_send.at[ch])


def hand_on(act_in, grad_in, act_out, grad_out, sem):
    copies = []
    for n, (src, dst) in enumerate(((act_in, act_out), (grad_in, grad_out))):
        size = src.shape[0] // 4
        for i in range(4):
            these = pl.ds(i * size, size)
            copies.append(pltpu.make_async_copy(src.at[these], dst.at[these], sem.at[n, i]))
    for copy in copies:
        copy.start()
    for copy in copies:
        copy.wait()


def solution(mesh):
    def local(tokens, weight, cotangent):
        rows, feats = tokens.shape
        depth, width = weight.shape
        n_row, n_col = mesh.shape["row"], mesh.shape["col"]
        chunks = len(WIDTHS)
        mid = rows // 2
        bf16, f32 = jnp.bfloat16, jnp.float32
        dma = pltpu.SemaphoreType.DMA
        results = pl.pallas_call(
            kernel,
            out_shape=(
                pltpu.VMEM((rows, width), bf16),
                pltpu.VMEM((rows, feats), bf16),
            ),
            in_specs=[pl.BlockSpec(memory_space=pl.ANY)] * 3,
            out_specs=(pl.BlockSpec(memory_space=pltpu.VMEM),) * 2,
            scratch_shapes=[
                pltpu.VMEM((rows, feats * n_col), bf16),
                tuple(pltpu.VMEM((depth * n_row, size), bf16) for size in WIDTHS),
                pltpu.VMEM((rows, width), bf16),
                pltpu.VMEM((rows, width), f32),
                pltpu.VMEM((rows, width), bf16),
                pltpu.VMEM((8, mid, feats), bf16),
                pltpu.VMEM((8, mid, feats), bf16),
                pltpu.VMEM((6, mid, feats), bf16),
                pltpu.VMEM((2, mid, feats), bf16),
                pltpu.VMEM((2, 2, mid, feats), bf16),
                pltpu.VMEM((2 * EARLY, mid, feats), f32),
                pltpu.VMEM((rows, feats), f32),
                pltpu.VMEM((mid, feats), f32),
                dma((3,)),
                dma((chunks,)),
                dma((chunks,)),
                dma((chunks, 2, 20)),
                dma,
                dma((8,)),
                dma((len(STEPS),)),
                dma((len(STEPS),)),
                dma((len(STEPS),)),
                dma((len(STEPS),)),
            ],
            compiler_params=pltpu.CompilerParams(
                collective_id=0, has_side_effects=True, vmem_limit_bytes=52 << 20
            ),
            cost_estimate=pl.CostEstimate(
                flops=4 * rows * feats * n_col * width, bytes_accessed=1 << 24, transcendentals=2 * rows * width
            ),
        )(tokens, weight, cotangent)
        return pl.pallas_call(
            hand_on,
            out_shape=tuple(jax.ShapeDtypeStruct(a.shape, a.dtype) for a in results),
            in_specs=[pl.BlockSpec(memory_space=pltpu.VMEM)] * 2,
            out_specs=(pl.BlockSpec(memory_space=pl.ANY),) * 2,
            scratch_shapes=[dma((2, 4))],
            compiler_params=pltpu.CompilerParams(vmem_limit_bytes=8 << 20),
        )(*results)

    in_specs = (P("row", "col"), P("row", "col"), P("row", "col"))
    out_specs = (P("row", "col"), P("row", "col"))
    return jax.shard_map(local, mesh=mesh, in_specs=in_specs, out_specs=out_specs, check_vma=False)
```
